32 devices in a mesh: parts: 2 (over x), node: 8 (over z, y), local: 2 (over core).
Axes of the slice: x: 2, y: 2, z: 4, core: 2. Of those that a mesh axis runs over, the one named last changes fastest.
Arguments:
- attn_partial: bfloat16 [2, 4096, 6144], P('local', ('parts', 'node')), parts along dimension 1, may hold values from -4 to 4
- residual: bfloat16 [4096, 6144], P(('parts', 'node', 'local')), parts along dimension 0, may hold values from -4 to 4
- norm_gain: float32 [6144], replicated, may hold values from 0.5 to 1.5
- expert_ids: int32 [4096, 4], P(('parts', 'node', 'local')), parts along dimension 0, may hold values from 0 to 7, all different within a row; in each aligned block of 128 rows (0 to 127, 128 to 255, ...) at most 96 rows name the same one
- gate_weights: float32 [4096, 4], P(('parts', 'node', 'local')), parts along dimension 0, may hold values from 0.05 to 0.45
- up_weight: bfloat16 [8, 6144, 1536], P('node', None, 'local'), may hold values from -0.078125 to 0.078125
- down_weight: bfloat16 [8, 1536, 6144], P('node', 'local'), may hold values from -0.15625 to 0.15625
Outputs:
- layer_out: bfloat16 [4096, 6144], P(('parts', 'node', 'local')), parts along dimension 0
The draws below stay inside these ranges and needn't reach their ends.
There are 2 independent parts, one for each index of `parts`. The reference program is written for one: setup_inputs(seed, part) draws one part's arguments, and reference() takes and returns one part's arrays. A program takes and returns all parts, laid end to end along the dimension named above; an argument that names none is the same for every part. Nothing has to cross between parts.
Inputs may be any that keep to these rules, and one draw needn't show every extreme that they name: `expert_ids`: each token names 4 different experts. Within each aligned block of 128 tokens (the tokens of one device) no expert is named by more than 96 tokens, and in every draw some expert is named by exactly 96 tokens of some block.
All inputs are finite; a program needn't handle non-finite values.
Results may differ from the reference program's by a relative error of at most 0.0095.
Values may be sent and summed in bfloat16 or wider, within the bound.
A program may use at most 192 MiB of HBM per device.

```python
import math
import jax
import jax.numpy as jnp
import numpy as np
from jax import lax

D = 6144
FF = 1536
TOP = 4
TOK_DEV = 128
TOKENS = 2048
EXPERTS = 8
CAP = 96
N_NODE = 8
N_LOCAL = 2


def level_of(key, extent, pieces, least, top_value):
    def one(axis_at, shards_of):
        steps = jax.random.uniform(jax.random.fold_in(jax.random.fold_in(key, 6), axis_at), (shards_of,), jnp.float32, least / len(pieces), top_value / len(pieces))
        return jnp.repeat(jnp.exp(steps), extent[axis_at] // shards_of).reshape((-1,) + (1,) * (len(extent) - axis_at - 1))

    level = one(*pieces[0])
    for cut in pieces[1:]:
        level = level * one(*cut)
    return level


def deal_out(key, own, number, rows, amount, top, bound, slope):
    order = jax.random.permutation(key, amount)
    heavy_load, common = shares(amount, rows * top, bound, slope, True), shares(amount, rows * top, bound, slope, False)
    places = jnp.arange(amount)

    def named(sizes, rotation):
        used = int((sizes > 0).sum())
        fixed = max(1, used // 4)
        shifted = fixed + (places - fixed + rotation * (used - fixed)) % max(1, amount - fixed)
        return jnp.zeros((amount,), jnp.int32).at[order[jnp.where(places < fixed, places, shifted)]].set(jnp.asarray(sizes, jnp.int32))

    sizes = jnp.where(number % 4 == 0, named(heavy_load, number // 4), named(common, number - number // 4 - 1))
    mixed = jax.random.permutation(jax.random.fold_in(own, 3), amount)
    donor, receiver = mixed[0:amount // 2 * 2:2], mixed[1:amount // 2 * 2:2]
    room = jnp.minimum(sizes[donor] - 1, bound - sizes[receiver]) // 2
    room = jnp.where((donor == order[0]) | (receiver == order[0]) | (sizes[receiver] == 0), 0, jnp.maximum(room, 0))
    shifted = jax.random.randint(jax.random.fold_in(own, 4), (amount // 2,), 0, 1 << 20) % (room + 1)
    sizes = sizes.at[donor].add(-shifted).at[receiver].add(shifted)
    members = jnp.searchsorted(jnp.cumsum(sizes), jnp.arange(rows * top), side="right").astype(jnp.int32)
    table = members.reshape(top, rows).T
    table = table[jax.random.permutation(jax.random.fold_in(own, 1), rows)]
    rotation = jax.random.randint(jax.random.fold_in(own, 2), (rows, 1), 0, top)
    return jnp.take_along_axis(table, (jnp.arange(top)[None, :] + rotation) % top, axis=1)


def shares(number_of, total, most, lean, full):
    loads = [(1 << 20) // math.isqrt(grade ** lean) + 1 for grade in range(1, number_of + 1)]
    largest = most if full else min(most, max(-(-total // number_of), total * loads[0] // sum(loads)))
    least = 1 if total - largest >= number_of - 1 else 0
    holding, surplus = [largest] + [least] * (number_of - 1), total - largest - least * (number_of - 1)
    while surplus > 0:
        free = [i for i in range(1, number_of) if holding[i] < largest] or [i for i in range(1, number_of) if holding[i] < most]
        whole, budget = sum([loads[i] for i in free]), surplus
        for i in free:
            extra = min(most - holding[i], max(1, budget * loads[i] // whole), surplus)
            holding[i] = holding[i] + extra
            surplus = surplus - extra
    return np.array(holding)


def scatter_about(stream_key, shape, spread, reach, shards=(), held_as=jnp.bfloat16):
    values = jax.random.normal(stream_key, shape, jnp.float32) * spread
    if len(shards) > 0:
        values = level_of(stream_key, shape, shards, -0.22, 0.18) * values
    return jnp.clip(values, min=-reach, max=reach).astype(held_as)


def setup_inputs(seed: int = 0, part: int = 0) -> dict:
    key_list = jax.random.split(jax.random.key(seed), 8)
    part_keys = jax.random.split(jax.random.fold_in(key_list[7], part), 8)
    attn_partial = scatter_about(part_keys[0], (N_LOCAL, TOKENS, D), 0.5, 4.0, ((0, 2), (1, 8)))
    residual = scatter_about(part_keys[1], (TOKENS, D), 0.5, 4.0, ((0, 16),))
    norm_gain = jnp.clip(1.0 + 0.1 * jax.random.normal(key_list[2], (D,), jnp.float32), 0.5, 1.5)
    expert_ids_keys = jax.random.split(jax.random.fold_in(part_keys[3], 1), TOKENS // TOK_DEV)
    expert_ids_turns = jax.random.permutation(jax.random.fold_in(part_keys[3], 3), TOKENS // TOK_DEV)
    expert_ids = jax.vmap(lambda own, number: deal_out(jax.random.fold_in(part_keys[3], 2), own, number, TOK_DEV, EXPERTS, TOP, CAP, 1))(expert_ids_keys, expert_ids_turns).reshape((TOKENS, TOP))
    gate_weights = jnp.clip(0.05 + 0.39999999 * jax.random.uniform(part_keys[4], (TOKENS, TOP), jnp.float32) ** level_of(part_keys[4], (TOKENS, TOP), ((0, 16),), -0.2, 0.2), 0.05, 0.45)
    up_weight = scatter_about(key_list[5], (EXPERTS, D, FF), D ** -0.5, 0.078125, ((0, 8), (2, 2)))
    down_weight = scatter_about(key_list[6], (EXPERTS, FF, D), FF ** -0.5, 0.15625, ((0, 8), (1, 2)))
    return {"attn_partial": attn_partial, "residual": residual, "norm_gain": norm_gain, "expert_ids": expert_ids, "gate_weights": gate_weights, "up_weight": up_weight, "down_weight": down_weight}


def expert_rows(expert, normed, flat_ids, up_weight, down_weight):
    most = N_NODE * N_LOCAL * CAP
    token_of = (jnp.arange(TOKENS * TOP, dtype=jnp.int32) // TOP).astype(jnp.int32)
    matches = flat_ids == expert
    positions = jnp.nonzero(matches, size=most, fill_value=0)[0].astype(jnp.int32)
    live_count = jnp.sum(matches.astype(jnp.int32))
    picked = normed[token_of[positions]]
    activated = jax.nn.silu(jnp.dot(picked, up_weight[expert], preferred_element_type=jnp.float32)).astype(jnp.bfloat16)
    hidden_width = FF // N_LOCAL
    running = jnp.zeros((most, D), jnp.float32)
    for block_index in range(N_LOCAL):
        start = block_index * hidden_width
        piece = jnp.dot(activated[:, start:start + hidden_width], down_weight[expert, start:start + hidden_width], preferred_element_type=jnp.float32).astype(jnp.bfloat16)
        running = running + lax.optimization_barrier(piece).astype(jnp.float32)
    is_valid = jnp.arange(most, dtype=jnp.int32) < live_count
    target = jnp.where(is_valid, positions, TOKENS * TOP).astype(jnp.int32)
    return (running.astype(jnp.bfloat16), target)

def reference(attn_partial, residual, norm_gain, expert_ids, gate_weights, up_weight, down_weight):
    hidden_state = residual.astype(jnp.float32) + lax.optimization_barrier(jnp.sum(attn_partial.astype(jnp.float32), axis=0))
    mean_square = lax.optimization_barrier(jnp.mean(hidden_state * hidden_state, axis=-1, keepdims=True))
    normed = (hidden_state * lax.rsqrt(mean_square + 1e-06) * norm_gain.astype(jnp.float32)).astype(jnp.bfloat16)
    flat_ids = expert_ids.reshape(-1)

    def per_expert(expert):
        return expert_rows(expert, normed, flat_ids, up_weight, down_weight)
    values, targets = lax.map(per_expert, jnp.arange(EXPERTS, dtype=jnp.int32))
    entries = jnp.zeros((TOKENS * TOP, D), jnp.bfloat16).at[targets.reshape(-1)].set(values.reshape(-1, D), mode='drop')
    combined = lax.optimization_barrier(jnp.sum(gate_weights.astype(jnp.float32)[:, :, None] * entries.reshape(TOKENS, TOP, D).astype(jnp.float32), axis=1))
    return (hidden_state + combined).astype(jnp.bfloat16)
```

```python
import jax
import jax.numpy as jnp
from jax import lax
from jax.sharding import PartitionSpec as P


def on_device(attn_partial, residual, norm_gain, expert_ids, gate_weights, up_weight, down_weight):
    up = lax.all_gather(up_weight[0], "local", axis=0)
    down = lax.all_gather(down_weight[0], "local", axis=0)
    attention = lax.psum_scatter(attn_partial, "local", scatter_dimension=1, tiled=True).astype(
        jnp.float32
    )[0]
    hidden_state = residual.astype(jnp.float32) + attention
    mean_square = jnp.mean(hidden_state * hidden_state, axis=-1, keepdims=True)
    normed = (hidden_state * lax.rsqrt(mean_square + 1e-06) * norm_gain).astype(jnp.bfloat16)
    expert_count = lax.axis_size("node")
    experts = jnp.arange(expert_count, dtype=jnp.int32)
    dense_gates = jnp.sum(
        jnp.where(expert_ids[:, :, None] == experts, gate_weights[:, :, None], 0.0), axis=1
    )
    gates = lax.all_gather(dense_gates, "node", axis=0, tiled=True)
    me = lax.axis_index("node")
    gate = jnp.sum(jnp.where(experts == me, gates, 0.0), axis=1, keepdims=True)
    rows = lax.all_gather(normed, "node", axis=0, tiled=True)
    total = 0.0
    for half in range(up.shape[0]):
        activated = jax.nn.silu(
            jnp.dot(rows, up[half], preferred_element_type=jnp.float32)
        ).astype(jnp.bfloat16)
        total = total + jnp.dot(activated, down[half], preferred_element_type=jnp.float32)
    weighted = (gate * total).astype(jnp.bfloat16)
    combined = lax.psum_scatter(weighted, "node", scatter_dimension=0, tiled=True)
    return (hidden_state + combined.astype(jnp.float32)).astype(jnp.bfloat16)


def solution(mesh):
    in_specs = (
        P("local", ("parts", "node"), None),
        P(("parts", "node", "local"), None),
        P(),
        P(("parts", "node", "local"), None),
        P(("parts", "node", "local"), None),
        P("node", None, "local"),
        P("node", "local", None),
    )
    out_specs = P(("parts", "node", "local"), None)
    return jax.shard_map(
        on_device, mesh=mesh, in_specs=in_specs, out_specs=out_specs, check_vma=False
    )
```

```python
import functools

import jax
import jax.numpy as jnp
from jax import lax
from jax.experimental import pallas as pl
from jax.experimental.pallas import tpu as pltpu
from jax.sharding import PartitionSpec as P

MESH = pl.DeviceIdType.MESH
CHUNKS = 6
TILE = 256
SLOTS = 3


def kernel(
    ring, columns, att, res, gain, gates, up, down, out, xs,
    up_v, down_v, att_in, hidden, x0, xv, act, rs_in, rs_out, g_in, g_col,
    ag_send, ag_recv, g_send, g_recv, rs_send, rs_recv, w_send, w_recv, att_sem, local_sem,
):
    f32, bf16 = jnp.float32, jnp.bfloat16
    rows, width = res.shape
    half = rows // 2
    chunk = width // CHUNKS
    split = up_v.shape[0]
    up_tiles = up_v.shape[2] // TILE
    deep = down_v.shape[1]
    line = ring // columns

    node = lax.axis_index("node")
    core = lax.axis_index("local")
    sibling = {"local": 1 - core}

    def node_at(place):
        if columns == 1:
            return place
        second = lax.div(place, line)
        return (place * (1 - second) + (ring - 1 - place) * second) * 2 + second

    if columns == 1:
        place = node
    else:
        z, y = lax.div(node, 2), lax.rem(node, 2)
        place = z * (1 - y) + (ring - 1 - z) * y
    ahead = ({"node": node_at(lax.rem(place + 1, ring))}, {"node": node_at(lax.rem(place + ring - 1, ring))})

    def part(h):
        return pl.ds(h * half, half)

    def remote(src, dst, send, recv, to):
        return pltpu.make_async_remote_copy(
            src_ref=src, dst_ref=dst, send_sem=send, recv_sem=recv, device_id=to, device_id_type=MESH
        )

    def rows_copy(h, s, src=None):
        src = xs.at[s, part(h)] if src is None else src
        return remote(src, xs.at[s + 1, part(h)], ag_send.at[h, s], ag_recv.at[h, s + 1], ahead[h])

    def gate_copy(h, s):
        return remote(g_in.at[h, s], g_in.at[h, s + 1], g_send.at[h, s], g_recv.at[h, s + 1], ahead[h])

    def sum_copy(h, c, s):
        now, then = lax.rem(s, 2), lax.rem(s + 1, SLOTS)
        return remote(
            rs_out.at[now, c, part(h)], rs_in.at[then, c, part(h)],
            rs_send.at[h, c, now], rs_recv.at[h, c, then], ahead[h],
        )

    barrier = pltpu.get_barrier_semaphore()
    for other in (sibling,) + ahead:
        pl.semaphore_signal(barrier, inc=1, device_id=other, device_id_type=MESH)
    pl.semaphore_wait(barrier, 3)

    att_copy = remote(
        att.at[0, pl.ds((1 - core) * rows, rows)], att_in, att_sem.at[0], att_sem.at[1], sibling
    )
    att_copy.start()
    own_att = pltpu.make_async_copy(att.at[0, pl.ds(core * rows, rows)], xv, local_sem.at[0])
    own_att.start()
    own_up = pltpu.make_async_copy(up.at[0], up_v.at[core], local_sem.at[1])
    own_down = pltpu.make_async_copy(down.at[0], down_v.at[core], local_sem.at[2])
    g_in[0, 0] = gates[...]
    g_in[1, 0] = gates[...]
    own_att.wait()
    att_copy.wait()
    up_copy = remote(up.at[0], up_v.at[core], w_send.at[0], w_recv.at[0], sibling)
    down_copy = remote(down.at[0], down_v.at[core], w_send.at[1], w_recv.at[1], sibling)
    up_copy.start()
    own_up.start()
    down_copy.start()
    own_down.start()

    for h in range(2):
        @pl.loop(0, half // 16)
        def _(i):
            at = pl.ds(pl.multiple_of(h * half + i * 16, 16), 16)
            state = res[at, :].astype(f32) + (xv[at, :].astype(f32) + att_in[at, :].astype(f32))
            hidden[at, :] = state
            mean_square = jnp.mean(state * state, axis=-1, keepdims=True)
            x0[at, :] = (state * lax.rsqrt(mean_square + 1e-06) * gain[...]).astype(bf16)

        gate_copy(h, 0).start()
        rows_copy(h, 0, x0.at[part(h)]).start()

    def take_gates(s):
        lane = lax.broadcasted_iota(jnp.int32, gates.shape, 1)
        expert = lax.broadcasted_iota(jnp.int32, gates.shape, 0)
        both = jnp.where(lane < half, g_in[0, s], g_in[1, s])
        row = jnp.sum(jnp.where(expert == node, both, 0.0), axis=0, keepdims=True)
        a = lax.broadcasted_iota(jnp.int32, (rows, rows), 0)
        b = lax.broadcasted_iota(jnp.int32, (rows, rows), 1)
        g_col[...] = jnp.sum(jnp.where(a == b, row, 0.0), axis=1, keepdims=True)

    def project_up(x):
        @pl.loop(0, split * up_tiles)
        def _(j):
            h, k = lax.div(j, up_tiles), lax.rem(j, up_tiles)
            v = jnp.dot(
                x[...], up_v[h, :, pl.ds(pl.multiple_of(k * TILE, TILE), TILE)],
                preferred_element_type=f32,
            )
            act[:, pl.ds(pl.multiple_of(j * TILE, TILE), TILE)] = (v / (1.0 + jnp.exp(-v))).astype(bf16)

    def project_down(at):
        total = jnp.dot(act[:, :deep], down_v[0, :, at], preferred_element_type=f32)
        for h in range(1, split):
            total = total + jnp.dot(
                act[:, h * deep:(h + 1) * deep], down_v[h, :, at], preferred_element_type=f32
            )
        return g_col[...] * total

    def arrive(s):
        for h in range(2):
            rows_copy(h, s - 1).wait_recv()
            gate_copy(h, s - 1).wait_recv()

            @pl.when(s < ring - 1)
            def _():
                gate_copy(h, s).start()
                rows_copy(h, s).start()

        load = pltpu.make_async_copy(xs.at[s], xv, local_sem.at[3])
        load.start()
        take_gates(s)
        load.wait()

    arrive(1)
    own_up.wait()
    up_copy.wait()
    project_up(xv)
    own_down.wait()
    down_copy.wait()

    def step(s, carry):
        now, slot = lax.rem(s, 2), lax.rem(s, SLOTS)

        def one(c, carry):
            @pl.when(s >= 2)
            def _():
                for h in range(2):
                    sum_copy(h, c, s - 1).wait_recv()

            @pl.when(s >= 3)
            def _():
                for h in range(2):
                    sum_copy(h, c, s - 2).wait_send()

            @pl.loop(0, chunk // TILE)
            def _(t):
                inner = pl.ds(pl.multiple_of(t * TILE, TILE), TILE)
                mine = project_down(pl.ds(pl.multiple_of(c * chunk + t * TILE, TILE), TILE))

                @pl.when(s >= 2)
                def _():
                    rs_out[now, c, :, inner] = (mine + rs_in[slot, c, :, inner].astype(f32)).astype(bf16)

                @pl.when(s < 2)
                def _():
                    rs_out[now, c, :, inner] = mine.astype(bf16)

            for h in range(2):
                sum_copy(h, c, s).start()
            return carry

        lax.fori_loop(0, CHUNKS, one, 0)

        @pl.when(s < ring - 1)
        def _():
            arrive(s + 1)
            project_up(xv)

        return carry

    lax.fori_loop(1, ring, step, 0)

    take_gates(0)
    project_up(x0)

    def last(c, carry):
        @pl.loop(0, chunk // TILE)
        def _(t):
            at = pl.ds(pl.multiple_of(c * chunk + t * TILE, TILE), TILE)
            hidden[:, at] = hidden[:, at] + project_down(at)

        return carry

    lax.fori_loop(0, CHUNKS, last, 0)

    def finish(c, carry):
        for h in range(2):
            sum_copy(h, c, jnp.int32(ring - 1)).wait_recv()

        @pl.loop(0, chunk // TILE)
        def _(t):
            inner = pl.ds(pl.multiple_of(t * TILE, TILE), TILE)
            at = pl.ds(pl.multiple_of(c * chunk + t * TILE, TILE), TILE)
            out[:, at] = (hidden[:, at] + rs_in[ring % SLOTS, c, :, inner].astype(f32)).astype(bf16)

        for h in range(2):
            sum_copy(h, c, jnp.int32(ring - 2)).wait_send()
            sum_copy(h, c, jnp.int32(ring - 1)).wait_send()
        return carry

    lax.fori_loop(0, CHUNKS, finish, 0)

    for h in range(2):
        rows_copy(h, 0, x0.at[part(h)]).wait_send()
        gate_copy(h, 0).wait_send()

    def drain(s, carry):
        for h in range(2):
            rows_copy(h, s).wait_send()
            gate_copy(h, s).wait_send()
        return carry

    lax.fori_loop(1, ring - 1, drain, 0)


def on_device(columns, attn_partial, residual, norm_gain, expert_ids, gate_weights, up_weight, down_weight):
    ring = lax.axis_size("node")
    split = lax.axis_size("local")
    rows, width = residual.shape
    part = up_weight.shape[2]
    bf16, f32 = jnp.bfloat16, jnp.float32
    experts = jnp.arange(ring, dtype=jnp.int32)
    gates = jnp.sum(
        jnp.where(expert_ids.T[:, None, :] == experts[None, :, None], gate_weights.T[:, None, :], 0.0),
        axis=0,
    )
    vmem = pl.BlockSpec(memory_space=pltpu.VMEM)
    anywhere = pl.BlockSpec(memory_space=pl.ANY)
    chunk = width // CHUNKS
    dma = pltpu.SemaphoreType.DMA
    layer_out, _ = pl.pallas_call(
        functools.partial(kernel, ring, columns),
        out_shape=(
            jax.ShapeDtypeStruct((rows, width), bf16),
            jax.ShapeDtypeStruct((ring, rows, width), bf16),
        ),
        in_specs=[anywhere, vmem, vmem, vmem, anywhere, anywhere],
        out_specs=(vmem, anywhere),
        scratch_shapes=[
            pltpu.VMEM((split, width, part), bf16),
            pltpu.VMEM((split, part, width), bf16),
            pltpu.VMEM((rows, width), bf16),
            pltpu.VMEM((rows, width), f32),
            pltpu.VMEM((rows, width), bf16),
            pltpu.VMEM((rows, width), bf16),
            pltpu.VMEM((rows, split * part), bf16),
            pltpu.VMEM((SLOTS, CHUNKS, rows, chunk), bf16),
            pltpu.VMEM((2, CHUNKS, rows, chunk), bf16),
            pltpu.VMEM((2, ring, ring, rows), f32),
            pltpu.VMEM((rows, 1), f32),
            dma((2, ring)),
            dma((2, ring)),
            dma((2, ring)),
            dma((2, ring)),
            dma((2, CHUNKS, 2)),
            dma((2, CHUNKS, SLOTS)),
            dma((2,)),
            dma((2,)),
            dma((2,)),
            dma((4,)),
        ],
        compiler_params=pltpu.CompilerParams(
            collective_id=0, has_side_effects=True, vmem_limit_bytes=62 * 1024 * 1024
        ),
        cost_estimate=pl.CostEstimate(
            flops=4 * ring * rows * width * part * split,
            bytes_accessed=2 * 2 * width * part,
            transcendentals=0,
        ),
    )(attn_partial, residual, norm_gain.reshape(1, width), gates, up_weight, down_weight)
    return layer_out


def solution(mesh):
    in_specs = (
        P("local", ("parts", "node"), None),
        P(("parts", "node", "local"), None),
        P(),
        P(("parts", "node", "local"), None),
        P(("parts", "node", "local"), None),
        P("node", None, "local"),
        P("node", "local", None),
    )
    out_specs = P(("parts", "node", "local"), None)
    columns = 2 if mesh.shape["parts"] == 2 else 1
    return jax.shard_map(
        functools.partial(on_device, columns), mesh=mesh, in_specs=in_specs, out_specs=out_specs,
        check_vma=False,
    )
```

```python
import functools

import jax
import jax.numpy as jnp
from jax import lax
from jax.experimental import pallas as pl
from jax.experimental.pallas import tpu as pltpu
from jax.sharding import PartitionSpec as P

MESH = pl.DeviceIdType.MESH
CHUNKS = 6
TILE = 256
SLOTS = 3
LEAD = 2
PASS_AT = 0
PIECES = 2


def kernel(
    ring, columns, att, res, gain, gates, up, down, out, xs,
    up_v, down_v, att_in, hidden, x0, xv, act, rs_in, rs_out, g_in, g_col,
    ag_send, ag_recv, g_send, g_recv, rs_send, rs_recv, w_send, w_recv,
    att_send, att_recv, first_send, first_recv, local_sem,
):
    f32, bf16 = jnp.float32, jnp.bfloat16
    rows, width = res.shape
    half = rows // 2
    chunk = width // CHUNKS
    split = up_v.shape[0]
    up_tiles = up_v.shape[2] // TILE
    deep = down_v.shape[1]
    line = ring // columns

    node = lax.axis_index("node")
    core = lax.axis_index("local")
    sibling = {"local": 1 - core}

    def node_at(place):
        if columns == 1:
            return place
        second = lax.div(place, line)
        return (place * (1 - second) + (ring - 1 - place) * second) * 2 + second

    if columns == 1:
        place = node
    else:
        z, y = lax.div(node, 2), lax.rem(node, 2)
        place = z * (1 - y) + (ring - 1 - z) * y
    ahead = ({"node": node_at(lax.rem(place + 1, ring))}, {"node": node_at(lax.rem(place + ring - 1, ring))})

    def part(h):
        return pl.ds(h * half, half)

    def remote(src, dst, send, recv, to):
        return pltpu.make_async_remote_copy(
            src_ref=src, dst_ref=dst, send_sem=send, recv_sem=recv, device_id=to, device_id_type=MESH
        )

    def rows_copy(h, s):
        return remote(xs.at[s, part(h)], xs.at[s + 1, part(h)], ag_send.at[h, s], ag_recv.at[h, s + 1], ahead[h])

    def gate_copy(h, s):
        return remote(g_in.at[h, s], g_in.at[h, s + 1], g_send.at[h, s], g_recv.at[h, s + 1], ahead[h])

    def sum_copy(h, c, s):
        now, then = lax.rem(s, 2), lax.rem(s + 1, SLOTS)
        return remote(
            rs_out.at[now, c, part(h)], rs_in.at[then, c, part(h)],
            rs_send.at[h, c, now], rs_recv.at[h, c, then], ahead[h],
        )

    barrier = pltpu.get_barrier_semaphore()
    for other in (sibling,) + ahead:
        pl.semaphore_signal(barrier, inc=1, device_id=other, device_id_type=MESH)
    pl.semaphore_wait(barrier, 3)

    piece = half // PIECES

    def att_copy(h, q):
        at = h * half + q * piece
        return remote(
            att.at[0, pl.ds((1 - core) * rows + at, piece)], att_in.at[pl.ds(at, piece)],
            att_send.at[h, q], att_recv.at[h, q], sibling,
        )

    def first_copy(h, q):
        at = pl.ds(h * half + q * piece, piece)
        return remote(x0.at[at], xs.at[1, at], first_send.at[h, q], first_recv.at[h, q], ahead[h])

    for q in range(PIECES):
        for h in range(2):
            att_copy(h, q).start()
    own_att = pltpu.make_async_copy(att.at[0, pl.ds(core * rows, rows)], xv, local_sem.at[0])
    own_att.start()
    own_up = pltpu.make_async_copy(up.at[0], up_v.at[core], local_sem.at[1])
    own_down = pltpu.make_async_copy(down.at[0], down_v.at[core], local_sem.at[2])
    g_in[0, 0] = gates[...]
    g_in[1, 0] = gates[...]
    up_copy = remote(up.at[0], up_v.at[core], w_send.at[0], w_recv.at[0], sibling)
    down_copy = remote(down.at[0], down_v.at[core], w_send.at[1], w_recv.at[1], sibling)
    own_att.wait()
    for q in range(PIECES):
        for h in range(2):
            att_copy(h, q).wait_recv()
            if q == PIECES - 1 and h == 1:
                up_copy.start()
                own_up.start()

            @pl.loop(0, piece // 16)
            def _(i):
                at = pl.ds(pl.multiple_of(h * half + q * piece + i * 16, 16), 16)
                state = res[at, :].astype(f32) + (xv[at, :].astype(f32) + att_in[at, :].astype(f32))
                hidden[at, :] = state
                mean_square = jnp.mean(state * state, axis=-1, keepdims=True)
                x0[at, :] = (state * lax.rsqrt(mean_square + 1e-06) * gain[...]).astype(bf16)

            first_copy(h, q).start()
            if q == 0:
                gate_copy(h, 0).start()
    down_copy.start()
    own_down.start()

    def take_gates(s):
        lane = lax.broadcasted_iota(jnp.int32, gates.shape, 1)
        expert = lax.broadcasted_iota(jnp.int32, gates.shape, 0)
        both = jnp.where(lane < half, g_in[0, s], g_in[1, s])
        row = jnp.sum(jnp.where(expert == node, both, 0.0), axis=0, keepdims=True)
        a = lax.broadcasted_iota(jnp.int32, (rows, rows), 0)
        b = lax.broadcasted_iota(jnp.int32, (rows, rows), 1)
        g_col[...] = jnp.sum(jnp.where(a == b, row, 0.0), axis=1, keepdims=True)

    def project_up(x):
        @pl.loop(0, split * up_tiles)
        def _(j):
            h, k = lax.div(j, up_tiles), lax.rem(j, up_tiles)
            v = jnp.dot(
                x[...], up_v[h, :, pl.ds(pl.multiple_of(k * TILE, TILE), TILE)],
                preferred_element_type=f32,
            )
            act[:, pl.ds(pl.multiple_of(j * TILE, TILE), TILE)] = (v / (1.0 + jnp.exp(-v))).astype(bf16)

    def project_down(at):
        total = jnp.dot(act[:, :deep], down_v[0, :, at], preferred_element_type=f32)
        for h in range(1, split):
            total = total + jnp.dot(
                act[:, h * deep:(h + 1) * deep], down_v[h, :, at], preferred_element_type=f32
            )
        return g_col[...] * total

    def pass_on(s):
        for h in range(2):
            gate_copy(h, s - 1).wait_recv()
            if isinstance(s, int) and s == 1:
                for q in range(PIECES):
                    first_copy(h, q).wait_recv()
            else:
                rows_copy(h, s - 1).wait_recv()

            @pl.when(s < ring - 1)
            def _():
                gate_copy(h, s).start()
                rows_copy(h, s).start()

    def load(s):
        block = pltpu.make_async_copy(xs.at[s], xv, local_sem.at[3])
        block.start()
        take_gates(s)
        block.wait()

    for s in range(1, LEAD + 1):
        pass_on(s)
    load(1)
    own_up.wait()
    up_copy.wait()
    project_up(xv)
    own_down.wait()
    down_copy.wait()

    def step(s, carry):
        now, slot = lax.rem(s, 2), lax.rem(s, SLOTS)

        def one(c, carry):
            @pl.when((c == PASS_AT) & (s < ring - LEAD))
            def _():
                pass_on(s + LEAD)

            @pl.when(s >= 2)
            def _():
                for h in range(2):
                    sum_copy(h, c, s - 1).wait_recv()

            @pl.when(s >= 3)
            def _():
                for h in range(2):
                    sum_copy(h, c, s - 2).wait_send()

            @pl.loop(0, chunk // TILE)
            def _(t):
                inner = pl.ds(pl.multiple_of(t * TILE, TILE), TILE)
                mine = project_down(pl.ds(pl.multiple_of(c * chunk + t * TILE, TILE), TILE))

                @pl.when(s >= 2)
                def _():
                    rs_out[now, c, :, inner] = (mine + rs_in[slot, c, :, inner].astype(f32)).astype(bf16)

                @pl.when(s < 2)
                def _():
                    rs_out[now, c, :, inner] = mine.astype(bf16)

            for h in range(2):
                sum_copy(h, c, s).start()
            return carry

        lax.fori_loop(0, CHUNKS, one, 0)

        @pl.when(s < ring - 1)
        def _():
            load(s + 1)
            project_up(xv)

        return carry

    lax.fori_loop(1, ring, step, 0)

    take_gates(0)
    project_up(x0)

    def last(c, carry):
        @pl.loop(0, chunk // TILE)
        def _(t):
            at = pl.ds(pl.multiple_of(c * chunk + t * TILE, TILE), TILE)
            hidden[:, at] = hidden[:, at] + project_down(at)

        return carry

    lax.fori_loop(0, CHUNKS, last, 0)

    def finish(c, carry):
        for h in range(2):
            sum_copy(h, c, jnp.int32(ring - 1)).wait_recv()

        @pl.loop(0, chunk // TILE)
        def _(t):
            inner = pl.ds(pl.multiple_of(t * TILE, TILE), TILE)
            at = pl.ds(pl.multiple_of(c * chunk + t * TILE, TILE), TILE)
            out[:, at] = (hidden[:, at] + rs_in[ring % SLOTS, c, :, inner].astype(f32)).astype(bf16)

        for h in range(2):
            sum_copy(h, c, jnp.int32(ring - 2)).wait_send()
            sum_copy(h, c, jnp.int32(ring - 1)).wait_send()
        return carry

    lax.fori_loop(0, CHUNKS, finish, 0)

    for h in range(2):
        for q in range(PIECES):
            att_copy(h, q).wait_send()
            first_copy(h, q).wait_send()
        gate_copy(h, 0).wait_send()

    def drain(s, carry):
        for h in range(2):
            rows_copy(h, s).wait_send()
            gate_copy(h, s).wait_send()
        return carry

    lax.fori_loop(1, ring - 1, drain, 0)


def on_device(columns, attn_partial, residual, norm_gain, expert_ids, gate_weights, up_weight, down_weight):
    ring = lax.axis_size("node")
    split = lax.axis_size("local")
    rows, width = residual.shape
    part = up_weight.shape[2]
    bf16, f32 = jnp.bfloat16, jnp.float32
    experts = jnp.arange(ring, dtype=jnp.int32)
    gates = jnp.sum(
        jnp.where(expert_ids.T[:, None, :] == experts[None, :, None], gate_weights.T[:, None, :], 0.0),
        axis=0,
    )
    vmem = pl.BlockSpec(memory_space=pltpu.VMEM)
    anywhere = pl.BlockSpec(memory_space=pl.ANY)
    chunk = width // CHUNKS
    dma = pltpu.SemaphoreType.DMA
    layer_out, _ = pl.pallas_call(
        functools.partial(kernel, ring, columns),
        out_shape=(
            jax.ShapeDtypeStruct((rows, width), bf16),
            jax.ShapeDtypeStruct((ring, rows, width), bf16),
        ),
        in_specs=[anywhere, vmem, vmem, vmem, anywhere, anywhere],
        out_specs=(vmem, anywhere),
        scratch_shapes=[
            pltpu.VMEM((split, width, part), bf16),
            pltpu.VMEM((split, part, width), bf16),
            pltpu.VMEM((rows, width), bf16),
            pltpu.VMEM((rows, width), f32),
            pltpu.VMEM((rows, width), bf16),
            pltpu.VMEM((rows, width), bf16),
            pltpu.VMEM((rows, split * part), bf16),
            pltpu.VMEM((SLOTS, CHUNKS, rows, chunk), bf16),
            pltpu.VMEM((2, CHUNKS, rows, chunk), bf16),
            pltpu.VMEM((2, ring, ring, rows), f32),
            pltpu.VMEM((rows, 1), f32),
            dma((2, ring)),
            dma((2, ring)),
            dma((2, ring)),
            dma((2, ring)),
            dma((2, CHUNKS, 2)),
            dma((2, CHUNKS, SLOTS)),
            dma((2,)),
            dma((2,)),
            dma((2, PIECES)),
            dma((2, PIECES)),
            dma((2, PIECES)),
            dma((2, PIECES)),
            dma((4,)),
        ],
        compiler_params=pltpu.CompilerParams(
            collective_id=0, has_side_effects=True, vmem_limit_bytes=62 * 1024 * 1024
        ),
        cost_estimate=pl.CostEstimate(
            flops=4 * ring * rows * width * part * split,
            bytes_accessed=2 * 2 * width * part,
            transcendentals=0,
        ),
    )(attn_partial, residual, norm_gain.reshape(1, width), gates, up_weight, down_weight)
    return layer_out


def solution(mesh):
    in_specs = (
        P("local", ("parts", "node"), None),
        P(("parts", "node", "local"), None),
        P(),
        P(("parts", "node", "local"), None),
        P(("parts", "node", "local"), None),
        P("node", None, "local"),
        P("node", "local", None),
    )
    out_specs = P(("parts", "node", "local"), None)
    columns = 2 if mesh.shape["parts"] == 2 else 1
    return jax.shard_map(
        functools.partial(on_device, columns), mesh=mesh, in_specs=in_specs, out_specs=out_specs,
        check_vma=False,
    )
```

```python
import functools

import jax
import jax.numpy as jnp
from jax import lax
from jax.experimental import pallas as pl
from jax.experimental.pallas import tpu as pltpu
from jax.sharding import PartitionSpec as P

MESH = pl.DeviceIdType.MESH
CHUNKS = 6
TILE = 256
SLOTS = 3
LEAD = 4
PASS_AT = 0
PIECES = 2


def kernel(
    ring, columns, att, res, gain, gates, up, down, out, xs,
    up_v, down_v, att_in, hidden, x0, xv, act, rs_in, rs_out, g_in, g_col,
    ag_send, ag_recv, g_send, g_recv, rs_send, rs_recv, w_send, w_recv,
    att_send, att_recv, first_send, first_recv, local_sem,
):
    f32, bf16 = jnp.float32, jnp.bfloat16
    rows, width = res.shape
    half = rows // 2
    chunk = width // CHUNKS
    split = up_v.shape[0]
    up_tiles = up_v.shape[2] // TILE
    deep = down_v.shape[1]
    line = ring // columns

    node = lax.axis_index("node")
    core = lax.axis_index("local")
    sibling = {"local": 1 - core}

    def node_at(place):
        if columns == 1:
            return place
        second = lax.div(place, line)
        return (place * (1 - second) + (ring - 1 - place) * second) * 2 + second

    if columns == 1:
        place = node
    else:
        z, y = lax.div(node, 2), lax.rem(node, 2)
        place = z * (1 - y) + (ring - 1 - z) * y
    ahead = ({"node": node_at(lax.rem(place + 1, ring))}, {"node": node_at(lax.rem(place + ring - 1, ring))})

    def part(h):
        return pl.ds(h * half, half)

    def remote(src, dst, send, recv, to):
        return pltpu.make_async_remote_copy(
            src_ref=src, dst_ref=dst, send_sem=send, recv_sem=recv, device_id=to, device_id_type=MESH
        )

    def rows_copy(h, s):
        return remote(xs.at[s, part(h)], xs.at[s + 1, part(h)], ag_send.at[h, s], ag_recv.at[h, s + 1], ahead[h])

    def gate_copy(h, s):
        return remote(g_in.at[h, s], g_in.at[h, s + 1], g_send.at[h, s], g_recv.at[h, s + 1], ahead[h])

    def sum_copy(h, c, s):
        now, then = lax.rem(s, 2), lax.rem(s + 1, SLOTS)
        return remote(
            rs_out.at[now, c, part(h)], rs_in.at[then, c, part(h)],
            rs_send.at[h, c, now], rs_recv.at[h, c, then], ahead[h],
        )

    barrier = pltpu.get_barrier_semaphore()
    for other in (sibling,) + ahead:
        pl.semaphore_signal(barrier, inc=1, device_id=other, device_id_type=MESH)
    pl.semaphore_wait(barrier, 3)

    piece = half // PIECES

    def att_copy(h, q):
        at = h * half + q * piece
        return remote(
            att.at[0, pl.ds((1 - core) * rows + at, piece)], att_in.at[pl.ds(at, piece)],
            att_send.at[h, q], att_recv.at[h, q], sibling,
        )

    def first_copy(h, q):
        at = pl.ds(h * half + q * piece, piece)
        return remote(x0.at[at], xs.at[1, at], first_send.at[h, q], first_recv.at[h, q], ahead[h])

    for q in range(PIECES):
        for h in range(2):
            att_copy(h, q).start()
    own_att = pltpu.make_async_copy(att.at[0, pl.ds(core * rows, rows)], xv, local_sem.at[0])
    own_att.start()
    own_up = pltpu.make_async_copy(up.at[0], up_v.at[core], local_sem.at[1])
    own_down = pltpu.make_async_copy(down.at[0], down_v.at[core], local_sem.at[2])
    g_in[0, 0] = gates[...]
    g_in[1, 0] = gates[...]
    up_copy = remote(up.at[0], up_v.at[core], w_send.at[0], w_recv.at[0], sibling)
    down_copy = remote(down.at[0], down_v.at[core], w_send.at[1], w_recv.at[1], sibling)
    own_att.wait()
    for q in range(PIECES):
        for h in range(2):
            att_copy(h, q).wait_recv()
            if q == PIECES - 1 and h == 1:
                up_copy.start()
                own_up.start()

            @pl.loop(0, piece // 16)
            def _(i):
                at = pl.ds(pl.multiple_of(h * half + q * piece + i * 16, 16), 16)
                state = res[at, :].astype(f32) + (xv[at, :].astype(f32) + att_in[at, :].astype(f32))
                hidden[at, :] = state
                mean_square = jnp.mean(state * state, axis=-1, keepdims=True)
                x0[at, :] = (state * lax.rsqrt(mean_square + 1e-06) * gain[...]).astype(bf16)

            first_copy(h, q).start()
            if q == 0:
                gate_copy(h, 0).start()
    down_copy.start()
    own_down.start()

    def take_gates(s):
        lane = lax.broadcasted_iota(jnp.int32, gates.shape, 1)
        expert = lax.broadcasted_iota(jnp.int32, gates.shape, 0)
        both = jnp.where(lane < half, g_in[0, s], g_in[1, s])
        row = jnp.sum(jnp.where(expert == node, both, 0.0), axis=0, keepdims=True)
        a = lax.broadcasted_iota(jnp.int32, (rows, rows), 0)
        b = lax.broadcasted_iota(jnp.int32, (rows, rows), 1)
        g_col[...] = jnp.sum(jnp.where(a == b, row, 0.0), axis=1, keepdims=True)

    def project_up(x):
        @pl.loop(0, split * up_tiles)
        def _(j):
            h, k = lax.div(j, up_tiles), lax.rem(j, up_tiles)
            v = jnp.dot(
                x[...], up_v[h, :, pl.ds(pl.multiple_of(k * TILE, TILE), TILE)],
                preferred_element_type=f32,
            )
            act[:, pl.ds(pl.multiple_of(j * TILE, TILE), TILE)] = (v / (1.0 + jnp.exp(-v))).astype(bf16)

    def project_down(at):
        total = jnp.dot(act[:, :deep], down_v[0, :, at], preferred_element_type=f32)
        for h in range(1, split):
            total = total + jnp.dot(
                act[:, h * deep:(h + 1) * deep], down_v[h, :, at], preferred_element_type=f32
            )
        return g_col[...] * total

    def pass_on(s):
        for h in range(2):
            gate_copy(h, s - 1).wait_recv()
            if isinstance(s, int) and s == 1:
                for q in range(PIECES):
                    first_copy(h, q).wait_recv()
            else:
                rows_copy(h, s - 1).wait_recv()

            @pl.when(s < ring - 1)
            def _():
                gate_copy(h, s).start()
                rows_copy(h, s).start()

    def load(s):
        block = pltpu.make_async_copy(xs.at[s], xv, local_sem.at[3])
        block.start()
        take_gates(s)
        block.wait()

    for s in range(1, LEAD + 1):
        pass_on(s)
    load(1)
    own_up.wait()
    up_copy.wait()
    project_up(xv)
    own_down.wait()
    down_copy.wait()

    def step(s, carry):
        now, slot = lax.rem(s, 2), lax.rem(s, SLOTS)

        def one(c, carry):
            @pl.when((c == PASS_AT) & (s < ring - LEAD))
            def _():
                pass_on(s + LEAD)

            @pl.when(s >= 2)
            def _():
                for h in range(2):
                    sum_copy(h, c, s - 1).wait_recv()

            @pl.when(s >= 3)
            def _():
                for h in range(2):
                    sum_copy(h, c, s - 2).wait_send()

            @pl.loop(0, chunk // TILE)
            def _(t):
                inner = pl.ds(pl.multiple_of(t * TILE, TILE), TILE)
                mine = project_down(pl.ds(pl.multiple_of(c * chunk + t * TILE, TILE), TILE))

                @pl.when(s >= 2)
                def _():
                    rs_out[now, c, :, inner] = (mine + rs_in[slot, c, :, inner].astype(f32)).astype(bf16)

                @pl.when(s < 2)
                def _():
                    rs_out[now, c, :, inner] = mine.astype(bf16)

            for h in range(2):
                sum_copy(h, c, s).start()
            return carry

        lax.fori_loop(0, CHUNKS, one, 0)

        @pl.when(s < ring - 1)
        def _():
            load(s + 1)
            project_up(xv)

        return carry

    lax.fori_loop(1, ring, step, 0)

    take_gates(0)
    project_up(x0)

    def last(c, carry):
        @pl.loop(0, chunk // TILE)
        def _(t):
            at = pl.ds(pl.multiple_of(c * chunk + t * TILE, TILE), TILE)
            hidden[:, at] = hidden[:, at] + project_down(at)

        return carry

    lax.fori_loop(0, CHUNKS, last, 0)

    def finish(c, carry):
        for h in range(2):
            sum_copy(h, c, jnp.int32(ring - 1)).wait_recv()

        @pl.loop(0, chunk // TILE)
        def _(t):
            inner = pl.ds(pl.multiple_of(t * TILE, TILE), TILE)
            at = pl.ds(pl.multiple_of(c * chunk + t * TILE, TILE), TILE)
            out[:, at] = (hidden[:, at] + rs_in[ring % SLOTS, c, :, inner].astype(f32)).astype(bf16)

        for h in range(2):
            sum_copy(h, c, jnp.int32(ring - 2)).wait_send()
            sum_copy(h, c, jnp.int32(ring - 1)).wait_send()
        return carry

    lax.fori_loop(0, CHUNKS, finish, 0)

    for h in range(2):
        for q in range(PIECES):
            att_copy(h, q).wait_send()
            first_copy(h, q).wait_send()
        gate_copy(h, 0).wait_send()

    def drain(s, carry):
        for h in range(2):
            rows_copy(h, s).wait_send()
            gate_copy(h, s).wait_send()
        return carry

    lax.fori_loop(1, ring - 1, drain, 0)


def on_device(columns, attn_partial, residual, norm_gain, expert_ids, gate_weights, up_weight, down_weight):
    ring = lax.axis_size("node")
    split = lax.axis_size("local")
    rows, width = residual.shape
    part = up_weight.shape[2]
    bf16, f32 = jnp.bfloat16, jnp.float32
    experts = jnp.arange(ring, dtype=jnp.int32)
    gates = jnp.sum(
        jnp.where(expert_ids.T[:, None, :] == experts[None, :, None], gate_weights.T[:, None, :], 0.0),
        axis=0,
    )
    vmem = pl.BlockSpec(memory_space=pltpu.VMEM)
    anywhere = pl.BlockSpec(memory_space=pl.ANY)
    chunk = width // CHUNKS
    dma = pltpu.SemaphoreType.DMA
    layer_out, _ = pl.pallas_call(
        functools.partial(kernel, ring, columns),
        out_shape=(
            jax.ShapeDtypeStruct((rows, width), bf16),
            jax.ShapeDtypeStruct((ring, rows, width), bf16),
        ),
        in_specs=[anywhere, vmem, vmem, vmem, anywhere, anywhere],
        out_specs=(vmem, anywhere),
        scratch_shapes=[
            pltpu.VMEM((split, width, part), bf16),
            pltpu.VMEM((split, part, width), bf16),
            pltpu.VMEM((rows, width), bf16),
            pltpu.VMEM((rows, width), f32),
            pltpu.VMEM((rows, width), bf16),
            pltpu.VMEM((rows, width), bf16),
            pltpu.VMEM((rows, split * part), bf16),
            pltpu.VMEM((SLOTS, CHUNKS, rows, chunk), bf16),
            pltpu.VMEM((2, CHUNKS, rows, chunk), bf16),
            pltpu.VMEM((2, ring, ring, rows), f32),
            pltpu.VMEM((rows, 1), f32),
            dma((2, ring)),
            dma((2, ring)),
            dma((2, ring)),
            dma((2, ring)),
            dma((2, CHUNKS, 2)),
            dma((2, CHUNKS, SLOTS)),
            dma((2,)),
            dma((2,)),
            dma((2, PIECES)),
            dma((2, PIECES)),
            dma((2, PIECES)),
            dma((2, PIECES)),
            dma((4,)),
        ],
        compiler_params=pltpu.CompilerParams(
            collective_id=0, has_side_effects=True, vmem_limit_bytes=62 * 1024 * 1024
        ),
        cost_estimate=pl.CostEstimate(
            flops=4 * ring * rows * width * part * split,
            bytes_accessed=2 * 2 * width * part,
            transcendentals=0,
        ),
    )(attn_partial, residual, norm_gain.reshape(1, width), gates, up_weight, down_weight)
    return layer_out


def solution(mesh):
    in_specs = (
        P("local", ("parts", "node"), None),
        P(("parts", "node", "local"), None),
        P(),
        P(("parts", "node", "local"), None),
        P(("parts", "node", "local"), None),
        P("node", None, "local"),
        P("node", "local", None),
    )
    out_specs = P(("parts", "node", "local"), None)
    columns = 2 if mesh.shape["parts"] == 2 else 1
    return jax.shard_map(
        functools.partial(on_device, columns), mesh=mesh, in_specs=in_specs, out_specs=out_specs,
        check_vma=False,
    )
```
